32 devices in a mesh: replica: 4 (over y, core), shard: 8 (over z, x).
Axes of the slice: x: 2, y: 2, z: 4, core: 2. Of those that a mesh axis runs over, the one named last changes fastest.
Arguments:
- tokens: bfloat16 [32768, 768], P(('replica', 'shard')), may hold values from -6 to 6
- segment: int32 [32768], P(('replica', 'shard')), may hold values from 0 to 11, as said below
- norm_gain: bfloat16 [768], P('shard'), may hold values from 0.099609375 to 1.8984375
- w_in: bfloat16 [768, 3352], P('shard'), may hold values from -0.21875 to 0.21875
- conv_w: bfloat16 [4, 1792], P(None, 'shard'), may hold values from -3 to 3
- conv_b: bfloat16 [1792], P('shard'), may hold values from -3 to 3
- dt_bias: float32 [24], replicated, may hold values from -6 to -3
- a_log: float32 [24], replicated, may hold values from -6 to 1.4
- d_skip: float32 [24], replicated, may hold values from 0.5 to 1.5
- gate_gain: bfloat16 [1536], P('shard'), may hold values from 0.099609375 to 1.8984375
- w_out: bfloat16 [1536, 768], P('shard'), may hold values from -0.15625 to 0.15625
- cotangent: bfloat16 [32768, 768], P(('replica', 'shard')), may hold values from -6 to 6
Outputs:
- block_out: bfloat16 [32768, 768], P(('replica', 'shard'))
- grad_tokens: float32 [32768, 768], P(('replica', 'shard'))
- grad_norm_gain: float32 [768], P('shard')
- grad_w_in: float32 [768, 3352], P('shard')
- grad_conv_w: float32 [4, 1792], P(None, 'shard')
- grad_conv_b: float32 [1792], P('shard')
- grad_dt_bias: float32 [24], replicated
- grad_a_log: float32 [24], replicated
- grad_d_skip: float32 [24], replicated
- grad_gate_gain: float32 [1536], P('shard')
- grad_w_out: float32 [1536, 768], P('shard')
The draws below stay inside these ranges and needn't reach their ends.
Inputs may be any that keep to these rules, and one draw needn't show every extreme that they name: `segment`: segment numbers start at 0 and rise by one at each new document, never falling, across all 32768 tokens. Each replica group's 8192 tokens begin a new document and are exactly 3 documents of 1024 to 4096 tokens packed back to back; each group holds one of exactly 4096 tokens.
All inputs are finite; a program needn't handle non-finite values.
Results may differ from the reference program's by a relative error of at most 0.019.
Values may be sent and summed in bfloat16 or wider, within the bound.
A program may use at most 192 MiB of HBM per device.

```python
from functools import partial
import jax
import jax.numpy as jnp
from jax import lax

D = 768
H = 24
P_SIZE = 64
N = 128
KC = 4
SPAN = 256
MIN_LEN = 1024
MAX_LEN = 4096
DI = 1536
CONV = 1792
IN_W = 3352
GROUP_TOK = 8192
DOCS = 3
TOKENS = 32768
N_REPLICA = 4


def draw_segment(key, part):
    key = jax.random.fold_in(key, 5)
    weight_key, pick_key = jax.random.split(key)
    doc_count = DOCS
    spare = GROUP_TOK - MAX_LEN - (doc_count - 1) * MIN_LEN
    picked = jax.random.randint(pick_key, (N_REPLICA, 1), 0, 2)
    columns = jnp.arange(doc_count, dtype=jnp.int32)[None, :]
    weights = jax.random.randint(weight_key, (N_REPLICA, doc_count), 3, 5)
    weights = jnp.where(columns == picked, 0, weights).astype(jnp.int32)
    total_weight = jnp.sum(weights, axis=1, keepdims=True)
    extra = spare * weights // total_weight
    leftover = spare - jnp.sum(extra, axis=1, keepdims=True)
    target = jnp.where(picked == doc_count - 1, 0, doc_count - 1)
    extra = extra + jnp.where(columns == target, leftover, 0)
    lengths = jnp.where(columns == picked, MAX_LEN, MIN_LEN + extra).astype(jnp.int32)
    ends = jnp.cumsum(lengths, axis=1)
    positions = jnp.arange(GROUP_TOK, dtype=jnp.int32)
    local_ids = jnp.sum((positions[None, :, None] >= ends[:, None, :]).astype(jnp.int32), axis=2)
    offsets = jnp.arange(N_REPLICA, dtype=jnp.int32)[:, None] * doc_count
    return (local_ids + offsets).astype(jnp.int32).reshape(TOKENS)


def draw_a_log(key, part):
    key = jax.random.fold_in(key, 11)
    pick_key, slow_key, fast_key = jax.random.split(key, 3)
    chooser = jax.random.uniform(pick_key, (H,))
    slow_rates = jax.random.uniform(slow_key, (H,), minval=-6.0, maxval=-4.0)
    fast_rates = jax.random.uniform(fast_key, (H,), minval=-0.5, maxval=1.4)
    share = 0.5
    return jnp.where(chooser < share, slow_rates, fast_rates).astype(jnp.float32)


def block_scale(stream_key, shape, cuts, smallest, high):
    factor_of = 1.0
    for axis_at, shards_of in cuts:
        heights = jax.random.uniform(jax.random.fold_in(jax.random.fold_in(stream_key, 6), axis_at), (shards_of,), jnp.float32, smallest / len(cuts), high / len(cuts))
        factor_of = factor_of * jnp.repeat(jnp.exp(heights), shape[axis_at] // shards_of).reshape((-1,) + (1,) * (len(shape) - 1 - axis_at))
    return factor_of


def normal_values(own_key, shape, spread, most, shards=(), held_as=jnp.bfloat16):
    drawn = jax.random.normal(own_key, shape, jnp.float32) * spread
    if len(shards) > 0:
        drawn = block_scale(own_key, shape, shards, -0.22, 0.18) * drawn
    return jnp.clip(drawn, min=-most, max=most).astype(held_as)


def setup_inputs(seed: int = 0) -> dict:
    streams_of = jax.random.split(jax.random.key(seed), 13)
    return {
        "tokens": normal_values(streams_of[0], (TOKENS, D), 1.0, 6.0, ((0, 32),)),
        "segment": draw_segment(jax.random.fold_in(streams_of[12], 71), 0),
        "norm_gain": jnp.clip(1.0 + 0.18 * jax.random.normal(streams_of[2], (D,), jnp.float32), 0.099609375, 1.8984375).astype(jnp.bfloat16),
        "w_in": normal_values(streams_of[3], (D, IN_W), D ** -0.5, 0.21875, ((0, 8),)),
        "conv_w": normal_values(streams_of[4], (KC, CONV), KC ** -0.5, 3.0, ((1, 8),)),
        "conv_b": normal_values(streams_of[5], (CONV,), 0.5, 3.0, ((0, 8),)),
        "dt_bias": jnp.clip(jax.random.uniform(streams_of[6], (H,), jnp.float32, -6.0, -3.0), -6.0, -3.0),
        "a_log": draw_a_log(jax.random.fold_in(streams_of[12], 71), 0),
        "d_skip": jnp.clip(jax.random.uniform(streams_of[8], (H,), jnp.float32, 0.5, 1.5), 0.5, 1.5),
        "gate_gain": jnp.clip(1.0 + 0.18 * jax.random.normal(streams_of[9], (DI,), jnp.float32), 0.099609375, 1.8984375).astype(jnp.bfloat16),
        "w_out": normal_values(streams_of[10], (DI, D), DI ** -0.5, 0.15625, ((0, 8),)),
        "cotangent": normal_values(streams_of[11], (TOKENS, D), 1.0, 6.0, ((0, 32),)),
    }


HIGHEST = lax.Precision.HIGHEST
EPSILON = 1e-05

@jax.custom_vjp
def low(v):
    return lax.optimization_barrier(v.astype(jnp.bfloat16)).astype(jnp.float32)

@jax.custom_vjp
def low_back(v):
    return v

def low_keep(v):
    return (low(v), None)

def low_pass(kept, grad):
    return (grad,)

def back_keep(v):
    return (v, None)

def back_low(kept, grad):
    return (low(grad),)
low.defvjp(low_keep, low_pass)
low_back.defvjp(back_keep, back_low)

def rms_scale(values, gain_vec):
    return values * lax.rsqrt(lax.optimization_barrier(jnp.mean(values * values, axis=-1, keepdims=True)) + EPSILON) * gain_vec

def causal_conv(xbc_in, rim_in, weight_in, bias_in, segment_ids, rim_segments):
    width = weight_in.shape[0]
    length = xbc_in.shape[0]
    row_block = jnp.concatenate([rim_in, xbc_in], axis=0)
    seg_block = jnp.concatenate([rim_segments, segment_ids], axis=0)
    summed = jnp.zeros_like(xbc_in) + bias_in[None, :]
    for offset in range(width):
        kept_mask = (seg_block[offset:offset + length] == segment_ids).astype(jnp.float32)
        summed = summed + weight_in[offset][None, :] * row_block[offset:offset + length] * kept_mask[:, None]
    return jax.nn.silu(summed)

def log_decay(raw_in, bias_in, alog_in):
    step_size = jax.nn.softplus(raw_in + bias_in[None, :])
    return (step_size, -jnp.exp(alog_in)[None, :] * step_size)

def gated_norm(mixed_in, gate_in, gain_in):
    product = mixed_in * jax.nn.silu(gate_in)
    return product * lax.rsqrt(lax.optimization_barrier(jnp.mean(product * product, axis=-1, keepdims=True)) + EPSILON) * gain_in[None, :]

def state_space(head_input, b_mat, c_mat, step_size, decay_rate, segment_ids, state_init, prev_segment, block_len):
    length, head_count, head_dim = head_input.shape
    block_count = length // block_len
    inputs = (head_input.reshape(block_count, block_len, head_count, head_dim), b_mat.reshape(block_count, block_len, -1), c_mat.reshape(block_count, block_len, -1), step_size.reshape(block_count, block_len, head_count), decay_rate.reshape(block_count, block_len, head_count), segment_ids.reshape(block_count, block_len))
    causal_mask = jnp.tril(jnp.ones((block_len, block_len), dtype=bool))

    def one_block(carry, block):
        state, last_segment = carry
        x_block, b_block, c_block, dt_block, a_block, s_block = block
        cumulative = jnp.cumsum(a_block, axis=0)
        same_doc = (s_block[:, None] == s_block[None, :]) & causal_mask
        decays = jnp.exp(jnp.where(same_doc[:, :, None], cumulative[:, None, :] - cumulative[None, :, :], -jnp.inf))
        scores = jnp.dot(c_block, b_block.T, precision=HIGHEST)
        scaled_x = x_block * dt_block[:, :, None]
        within = jnp.einsum('tsh,shp->thp', decays * scores[:, :, None], scaled_x, precision=HIGHEST)
        entering = jnp.exp(cumulative) * (s_block == last_segment).astype(jnp.float32)[:, None]
        from_state = jnp.einsum('tn,hpn->thp', c_block, state, precision=HIGHEST) * entering[:, :, None]
        leaving = jnp.exp(cumulative[-1][None, :] - cumulative) * (s_block == s_block[-1]).astype(jnp.float32)[:, None]
        passing = jnp.exp(cumulative[-1]) * (s_block[-1] == last_segment).astype(jnp.float32)
        new_state = state * passing[:, None, None] + jnp.einsum('sh,sn,shp->hpn', leaving, b_block, scaled_x, precision=HIGHEST)
        return ((new_state, s_block[-1]), within + from_state)
    (final_state, last_seen), outputs = lax.scan(jax.checkpoint(one_block), (state_init, prev_segment), inputs)
    return (outputs.reshape(length, head_count, head_dim), final_state)

def layer(segment, tokens, norm_gain, w_in, conv_w, conv_b, dt_bias, a_log, d_skip, gate_gain, w_out):
    normed = low(rms_scale(tokens, norm_gain[None, :]))
    projected = low(low_back(jnp.dot(normed, w_in, precision=HIGHEST)))
    gate_z = projected[:, :DI]
    xbc_part = projected[:, DI:DI + CONV]
    dt_raw = projected[:, DI + CONV:]
    rim_rows = jnp.zeros((KC - 1, CONV), jnp.float32)
    rim_segments = jnp.full((KC - 1,), -1, jnp.int32)
    conv_out = low(causal_conv(xbc_part, rim_rows, conv_w, conv_b, segment, rim_segments))
    head_input = conv_out[:, :DI].reshape(conv_out.shape[0], H, P_SIZE)
    b_mat = conv_out[:, DI:DI + N]
    c_mat = conv_out[:, DI + N:]
    step_size, decay_rate = log_decay(dt_raw, dt_bias, a_log)
    state_init = jnp.zeros((H, P_SIZE, N), jnp.float32)
    mixed_out, final_state = state_space(head_input, b_mat, c_mat, step_size, decay_rate, segment, state_init, jnp.int32(-1), SPAN)
    mixed_out = mixed_out + d_skip[None, :, None] * head_input
    gated_out = low(gated_norm(mixed_out.reshape(mixed_out.shape[0], DI), gate_z, gate_gain))
    return tokens + jnp.dot(gated_out, w_out, precision=HIGHEST)

def reference(tokens, segment, norm_gain, w_in, conv_w, conv_b, dt_bias, a_log, d_skip, gate_gain, w_out, cotangent):
    floats = tuple((member.astype(jnp.float32) for member in (tokens, norm_gain, w_in, conv_w, conv_b, dt_bias, a_log, d_skip, gate_gain, w_out)))
    result, pull_back = jax.vjp(partial(layer, segment), *floats)
    gradients = pull_back(cotangent.astype(jnp.float32))
    return (result.astype(jnp.bfloat16), gradients[0], gradients[1], gradients[2], gradients[3], gradients[4], gradients[5], gradients[6], gradients[7], gradients[8], gradients[9])
```

```python
import jax
import jax.numpy as jnp
from jax import lax
from jax.experimental import pallas as pl
from jax.experimental.pallas import tpu as pltpu
from jax.sharding import PartitionSpec as P

H = 24
P_SIZE = 64
N = 128
KC = 4
SPAN = 256
DI = 1536
CONV = 1792


EPSILON = 1e-05
WRAP_IDS = 256


def passed_along(shard, axis, by):
    count = lax.axis_size(axis)
    pairs = [(i, i + by) for i in range(count) if 0 <= i + by < count]
    return lax.ppermute(shard, axis, pairs)


def rms_scale(values, gain_vec):
    return (
        values * lax.rsqrt(jnp.mean(values * values, axis=-1, keepdims=True) + EPSILON) * gain_vec
    )


def causal_conv(xbc_in, rim_in, weight_in, bias_in, segment_ids, rim_segments):
    width = weight_in.shape[0]
    length = xbc_in.shape[0]
    row_block = jnp.concatenate([rim_in, xbc_in], axis=0)
    seg_block = jnp.concatenate([rim_segments, segment_ids], axis=0)
    summed = jnp.zeros_like(xbc_in) + bias_in[None, :]
    for offset in range(width):
        kept_mask = (seg_block[offset : offset + length] == segment_ids).astype(jnp.float32)
        summed = (
            summed
            + weight_in[offset][None, :] * row_block[offset : offset + length] * kept_mask[:, None]
        )
    return jax.nn.silu(summed)


def log_decay(raw_in, bias_in, alog_in):
    step_size = jax.nn.softplus(raw_in + bias_in[None, :])
    return (step_size, -jnp.exp(alog_in)[None, :] * step_size)


def gated_norm(mixed_in, gate_in, gain_in):
    product = mixed_in * jax.nn.silu(gate_in)
    return (
        product
        * lax.rsqrt(jnp.mean(product * product, axis=-1, keepdims=True) + EPSILON)
        * gain_in[None, :]
    )


MASKED = -1e30
HIGH = lax.Precision.HIGHEST


def mm(a, b, dims):
    return lax.dot_general(
        a.astype(jnp.bfloat16),
        b.astype(jnp.bfloat16),
        (dims, ((), ())),
        preferred_element_type=jnp.float32,
    )


NN = ((1,), (0,))
NT = ((1,), (1,))
TN = ((0,), (0,))


def block_mask(segc_ref, segr_ref):
    span = segc_ref.shape[0]
    at = lax.broadcasted_iota(jnp.int32, (span, span), 0)
    of = lax.broadcasted_iota(jnp.int32, (span, span), 1)
    keep = (segc_ref[:, 0:1] == segr_ref[0:1, :]) & (at >= of)
    return jnp.where(keep, 0.0, MASKED)


def pair_columns(cols, first):
    lane = lax.broadcasted_iota(jnp.int32, (cols.shape[0], 2 * P_SIZE), 1)
    return jnp.where(lane < P_SIZE, cols[:, first : first + 1], cols[:, first + 1 : first + 2])


def forward_kernel(
    conv_ref, cols_ref, rows_ref, segc_ref, segr_ref, skip_ref,
    mixed_ref, enter_ref, final_ref, state, bias, scores,
):
    span = conv_ref.shape[0]
    pairs = cols_ref.shape[0]
    wide = 2 * P_SIZE

    @pl.when(pl.program_id(0) == 0)
    def _():
        state[...] = jnp.zeros_like(state)

    b_mat = conv_ref[:, DI : DI + N]
    c_mat = conv_ref[:, DI + N :]
    bias[...] = block_mask(segc_ref, segr_ref)
    scores[...] = mm(c_mat, b_mat, NT)
    enter_ref[0] = state[...]
    lane = lax.broadcasted_iota(jnp.int32, (span, wide), 1)

    @pl.loop(0, pairs)
    def _(j):
        at = pl.ds(pl.multiple_of(j * wide, wide), wide)
        cols = cols_ref[j]
        xs = conv_ref[:, at].astype(jnp.float32)
        x = xs * pair_columns(cols, 2)
        xb = x.astype(jnp.bfloat16)
        parts = []
        for a in range(2):
            gaps = cols[:, a : a + 1] - rows_ref[j, a : a + 1, :]
            w = jnp.exp(gaps + bias[...]) * scores[...]
            parts.append(mm(w, xb, NN))
        within = jnp.where(lane < P_SIZE, parts[0], parts[1])
        enter = pair_columns(cols, 4)
        old = state[at, :]
        from_state = mm(c_mat, old, NT) * enter
        mixed_ref[:, at] = within + from_state + skip_ref[:, at] * xs
        leave = pair_columns(cols, 6)
        sub = lax.broadcasted_iota(jnp.int32, (wide, N), 0)
        passing = jnp.where(sub < P_SIZE, cols[span - 1 :, 4:5], cols[span - 1 :, 5:6])
        state[at, :] = old * passing + mm(x * leave, b_mat, TN)

    final_ref[...] = state[...]


def backward_kernel(
    conv_ref, gmix_ref, cols_ref, rows_ref, segc_ref, segr_ref, skip_ref, enter_ref, gout_ref,
    gconv_ref, gcols_ref, grows_ref, gskip_ref, gstate, bias, scores, gscores, gbc,
):
    span = conv_ref.shape[0]
    pairs = cols_ref.shape[0]
    wide = 2 * P_SIZE

    @pl.when(pl.program_id(0) == 0)
    def _():
        gstate[...] = gout_ref[...]
        gskip_ref[...] = jnp.zeros_like(gskip_ref)

    b_mat = conv_ref[:, DI : DI + N]
    c_mat = conv_ref[:, DI + N :]
    bias[...] = block_mask(segc_ref, segr_ref)
    scores[...] = mm(c_mat, b_mat, NT)
    gscores[...] = jnp.zeros_like(gscores)
    gbc[...] = jnp.zeros_like(gbc)
    lane = lax.broadcasted_iota(jnp.int32, (span, wide), 1)
    low = lane < P_SIZE
    low_sub = lax.broadcasted_iota(jnp.int32, (wide, N), 0) < P_SIZE
    last = lax.broadcasted_iota(jnp.int32, (span, 1), 0) == span - 1
    lane8 = lax.broadcasted_iota(jnp.int32, (span, 8), 1)

    @pl.loop(0, pairs)
    def _(j):
        at = pl.ds(pl.multiple_of(j * wide, wide), wide)
        cols = cols_ref[j]
        xs = conv_ref[:, at].astype(jnp.float32)
        dt = pair_columns(cols, 2)
        x = xs * dt
        xb = x.astype(jnp.bfloat16)
        gy = gmix_ref[:, at]
        gyb = gy.astype(jnp.bfloat16)
        parts = []
        row_sums = []
        for a in range(2):
            gaps = cols[:, a : a + 1] - rows_ref[j, a : a + 1, :]
            e = jnp.exp(gaps + bias[...])
            w = e * scores[...]
            mine = low if a == 0 else jnp.logical_not(low)
            dw = mm(jnp.where(mine, gy, 0.0), xb, NT)
            gscores[...] += e * dw
            q = w * dw
            row_sums.append(jnp.sum(q, axis=1, keepdims=True))
            grows_ref[j, a : a + 1, :] = jnp.sum(q, axis=0, keepdims=True)
            parts.append(mm(w, gyb, TN))
        gx = jnp.where(low, parts[0], parts[1])
        enter = pair_columns(cols, 4)
        leave = pair_columns(cols, 6)
        old = enter_ref[0, at, :]
        late = gstate[at, :]
        gye = gy * enter
        from_state = mm(c_mat, old, NT)
        gx_late = mm(b_mat, late, NT) * leave
        gbc[:, N:] += mm(gye, old, NN)
        gbc[:, :N] += mm(x * leave, late, NN)
        gx = gx + gx_late
        late_term = x * gx_late
        v1 = gye * from_state - late_term
        v2 = gx * xs
        passing = jnp.where(low_sub, cols[span - 1 :, 4:5], cols[span - 1 :, 5:6])
        through = late * passing
        kept = jnp.sum(through * old, axis=1, keepdims=True)
        ends = jnp.sum(late_term, axis=0, keepdims=True)
        low_row = lax.broadcasted_iota(jnp.int32, (1, wide), 1) < P_SIZE
        out = jnp.zeros((span, 8), jnp.float32)
        for a in range(2):
            mine = low if a == 0 else jnp.logical_not(low)
            mine_row = low_row if a == 0 else jnp.logical_not(low_row)
            tail = jnp.sum(jnp.where(mine_row, ends, 0.0), axis=1, keepdims=True)
            tail = tail + jnp.sum(
                kept[a * P_SIZE : (a + 1) * P_SIZE], axis=0, keepdims=True
            )
            gcum = row_sums[a] + jnp.sum(jnp.where(mine, v1, 0.0), axis=1, keepdims=True)
            gcum = gcum + jnp.where(last, tail, 0.0)
            gdt = jnp.sum(jnp.where(mine, v2, 0.0), axis=1, keepdims=True)
            out = jnp.where(lane8 == a, gcum, out)
            out = jnp.where(lane8 == 2 + a, gdt, out)
        gcols_ref[j] = out
        gskip_ref[:, at] += jnp.sum(gy * xs, axis=0, keepdims=True)
        gconv_ref[:, at] = gx * dt + skip_ref[:, at] * gy
        gstate[at, :] = through + mm(gye, c_mat, TN)

    gs = gscores[...].astype(jnp.bfloat16)
    gconv_ref[:, DI : DI + N] = gbc[:, :N] + mm(gs, c_mat, TN)
    gconv_ref[:, DI + N :] = gbc[:, N:] + mm(gs, b_mat, NN)


def scan_specs(count, order):
    pairs = H // 2
    return dict(
        conv=pl.BlockSpec((SPAN, CONV), lambda i: (order(i), 0)),
        mix=pl.BlockSpec((SPAN, DI), lambda i: (order(i), 0)),
        cols=pl.BlockSpec((pairs, SPAN, 8), lambda i: (0, order(i), 0)),
        rows=pl.BlockSpec((pairs, 2, SPAN), lambda i: (0, 0, order(i))),
        segc=pl.BlockSpec((SPAN, 1), lambda i: (order(i), 0)),
        segr=pl.BlockSpec((1, SPAN), lambda i: (0, order(i))),
        skip=pl.BlockSpec((1, DI), lambda i: (0, 0)),
        state=pl.BlockSpec((DI, N), lambda i: (0, 0)),
        states=pl.BlockSpec((1, DI, N), lambda i: (order(i), 0, 0)),
    )


def scan_forward(conv_b, cols, rows, segc, segr, skip):
    length = conv_b.shape[0]
    count = length // SPAN
    s = scan_specs(count, lambda i: i)
    f32 = jnp.float32
    return pl.pallas_call(
        forward_kernel,
        grid=(count,),
        in_specs=[s["conv"], s["cols"], s["rows"], s["segc"], s["segr"], s["skip"]],
        out_specs=[s["mix"], s["states"], s["state"]],
        out_shape=[
            jax.ShapeDtypeStruct((length, DI), f32),
            jax.ShapeDtypeStruct((count, DI, N), f32),
            jax.ShapeDtypeStruct((DI, N), f32),
        ],
        scratch_shapes=[
            pltpu.VMEM((DI, N), f32),
            pltpu.VMEM((SPAN, SPAN), f32),
            pltpu.VMEM((SPAN, SPAN), f32),
        ],
        compiler_params=pltpu.CompilerParams(vmem_limit_bytes=48 << 20),
    )(conv_b, cols, rows, segc, segr, skip)


def scan_backward(conv_b, g_mixed, cols, rows, segc, segr, skip, states, g_out):
    length = conv_b.shape[0]
    count = length // SPAN
    s = scan_specs(count, lambda i: count - 1 - i)
    f32 = jnp.float32
    return pl.pallas_call(
        backward_kernel,
        grid=(count,),
        in_specs=[
            s["conv"], s["mix"], s["cols"], s["rows"], s["segc"], s["segr"], s["skip"],
            s["states"], s["state"],
        ],
        out_specs=[s["conv"], s["cols"], s["rows"], s["skip"]],
        out_shape=[
            jax.ShapeDtypeStruct((length, CONV), f32),
            jax.ShapeDtypeStruct(cols.shape, f32),
            jax.ShapeDtypeStruct(rows.shape, f32),
            jax.ShapeDtypeStruct((1, DI), f32),
        ],
        scratch_shapes=[
            pltpu.VMEM((DI, N), f32),
            pltpu.VMEM((SPAN, SPAN), f32),
            pltpu.VMEM((SPAN, SPAN), f32),
            pltpu.VMEM((SPAN, SPAN), f32),
            pltpu.VMEM((SPAN, 2 * N), f32),
        ],
        compiler_params=pltpu.CompilerParams(vmem_limit_bytes=48 << 20),
    )(conv_b, g_mixed, cols, rows, segc, segr, skip, states, g_out)


def carried(state, gain, reverse):
    count, mine = (lax.axis_size("shard"), lax.axis_index("shard"))
    sent = jnp.concatenate(
        [state, jnp.pad(gain[None, :], ((0, 15), (0, N - H)))], axis=0
    ).astype(jnp.bfloat16)
    everything = lax.all_gather(sent, "shard")
    gains = everything[:, DI, :H].astype(jnp.float32)
    weights = [None] * count
    run = jnp.ones((H,), jnp.float32)
    for k in range(count) if reverse else reversed(range(count)):
        counts = k > mine if reverse else k < mine
        weights[k] = jnp.where(counts, run, 0.0)
        run = jnp.where(counts, run * gains[k], run)
    total = jnp.zeros((H, P_SIZE, N), jnp.float32)
    for k in range(count):
        total = total + weights[k][:, None, None] * everything[k, :DI].reshape(
            H, P_SIZE, N
        ).astype(jnp.float32)
    return total.reshape(DI, N)


def gather_params(w_in, w_out, conv_w, conv_b, norm_gain, gate_gain):
    parts = lax.axis_size("replica")
    mine = lax.axis_index("replica")

    def whole(w):
        rows = w.shape[0] // parts
        part = lax.dynamic_slice_in_dim(w, mine * rows, rows, 0)
        return lax.all_gather(part, ("shard", "replica"), axis=0, tiled=True)

    small = jnp.concatenate([conv_w.reshape(-1), conv_b, norm_gain, gate_gain])
    small = lax.all_gather(small, "shard", axis=0)
    count = small.shape[0]
    a = conv_w.size
    b = a + conv_b.size
    c = b + norm_gain.size
    full_conv = small[:, :a].reshape(count, KC, -1).transpose(1, 0, 2).reshape(KC, -1)
    return (
        whole(w_in),
        whole(w_out),
        full_conv.astype(jnp.float32),
        small[:, a:b].reshape(-1).astype(jnp.float32),
        small[:, b:c].reshape(-1).astype(jnp.float32),
        small[:, c:].reshape(-1).astype(jnp.float32),
    )


def owned_sum(g):
    part = lax.psum_scatter(
        g.astype(jnp.bfloat16), ("shard", "replica"), scatter_dimension=0, tiled=True
    )
    return lax.all_gather(part, "replica", axis=0, tiled=True).astype(jnp.float32)


def body(
    tokens,
    segment,
    norm_gain,
    w_in,
    conv_w,
    conv_b,
    dt_bias,
    a_log,
    d_skip,
    gate_gain,
    w_out,
    cotangent,
):
    full_in, full_out, full_conv, full_bias, full_norm, full_gate = gather_params(
        w_in, w_out, conv_w, conv_b, norm_gain, gate_gain
    )
    rim_len = KC - 1
    wrapped = segment % WRAP_IDS
    tok_f = tokens.astype(jnp.float32)
    count = tokens.shape[0]
    blocks = count // SPAN

    def norm_piece(tok_in, gain_in):
        return rms_scale(tok_in, gain_in[None, :])

    normed, norm_pull = jax.vjp(norm_piece, tok_f, full_norm)
    normed_b = normed.astype(jnp.bfloat16)
    projected = jnp.dot(normed_b, full_in, preferred_element_type=jnp.float32).astype(jnp.bfloat16)
    xbc_b = projected[:, DI : DI + CONV]
    rim = jnp.concatenate(
        [
            xbc_b[-rim_len:],
            jnp.broadcast_to(wrapped[-rim_len:, None].astype(jnp.bfloat16), (rim_len, N)),
        ],
        axis=1,
    )
    rim = passed_along(rim, "shard", 1)
    rim_rows = rim[:, :CONV]
    prev_segs = rim[:, CONV].astype(jnp.int32)
    prev_last = jnp.where(lax.axis_index("shard") == 0, 0, prev_segs[-1])
    xbc_f = xbc_b.astype(jnp.float32)
    rim_f = rim_rows.astype(jnp.float32)
    gate_z = projected[:, :DI].astype(jnp.float32)
    dt_raw = projected[:, DI + CONV :].astype(jnp.float32)

    def conv_piece(xbc_in, rim_in, weight_in, bias_in):
        return causal_conv(xbc_in, rim_in, weight_in, bias_in, wrapped, prev_segs)

    conv_out, conv_pull = jax.vjp(conv_piece, xbc_f, rim_f, full_conv, full_bias)
    conv_bf = conv_out.astype(jnp.bfloat16)

    step, decay = log_decay(dt_raw, dt_bias, a_log)
    decay_blocks = decay.reshape(blocks, SPAN, H)
    lower = jnp.tril(jnp.ones((SPAN, SPAN), jnp.float32))
    cum_blocks = jnp.einsum("ts,bsh->bth", lower, decay_blocks, precision=HIGH)
    seg_blocks = wrapped.reshape(blocks, SPAN)
    ends = seg_blocks[:, -1]
    before = jnp.concatenate([prev_last[None], ends[:-1]])
    at_last = cum_blocks[:, -1:]
    enter = jnp.exp(cum_blocks) * (seg_blocks == before[:, None]).astype(jnp.float32)[:, :, None]
    leave = (
        jnp.exp(at_last - cum_blocks)
        * (seg_blocks == ends[:, None]).astype(jnp.float32)[:, :, None]
    )
    before_sum = [jnp.zeros((H,), jnp.float32)]
    for b in range(blocks):
        before_sum.append(before_sum[-1] + cum_blocks[b, -1])
    base = jnp.stack(before_sum[:-1])
    running = (
        jnp.exp(cum_blocks + base[:, None, :]).reshape(count, H)
        * (wrapped == prev_last).astype(jnp.float32)[:, None]
    )
    carry_gain = running[-1]
    entering_gain = jnp.concatenate(
        [jnp.ones((1, H), jnp.float32), running.reshape(blocks, SPAN, H)[:-1, -1]]
    )

    pairs = H // 2
    cols = jnp.stack(
        [cum_blocks.reshape(count, H), step, enter.reshape(count, H), leave.reshape(count, H)],
        axis=1,
    )
    cols = cols.reshape(count, 4, pairs, 2).transpose(2, 0, 1, 3).reshape(pairs, count, 8)
    rows = cum_blocks.reshape(count, pairs, 2).transpose(1, 2, 0)
    segc = wrapped[:, None]
    segr = wrapped[None, :]
    skip = jnp.repeat(d_skip, P_SIZE)[None, :]

    local_mixed, local_states, local_state = scan_forward(conv_bf, cols, rows, segc, segr, skip)
    state_in = carried(local_state, carry_gain, False)
    c_mat = conv_bf[:, DI + N :]
    running_wide = jnp.repeat(running, P_SIZE, axis=1)
    mixed_out = local_mixed + mm(c_mat, state_in, NT) * running_wide
    gated_out, gate_pull = jax.vjp(gated_norm, mixed_out, gate_z, full_gate)
    gated_b = gated_out.astype(jnp.bfloat16)
    branch = jnp.dot(gated_b, full_out, preferred_element_type=jnp.float32)
    block_out = (tok_f + branch).astype(jnp.bfloat16)

    g_gated = mm(cotangent, full_out, NT)
    grad_out_full = mm(gated_b, cotangent, TN)
    part_out = owned_sum(grad_out_full)
    g_mixed, g_gate_z, g_gate_gain = gate_pull(g_gated)
    seed_grad = mm(g_mixed * running_wide, c_mat, TN)
    state_out_grad = carried(seed_grad, carry_gain, True)
    states = (
        local_states
        + jnp.repeat(entering_gain, P_SIZE, axis=1)[:, :, None] * state_in[None]
    )
    g_conv, g_cols, g_rows, g_skip = scan_backward(
        conv_bf, g_mixed, cols, rows, segc, segr, skip, states, state_out_grad
    )
    g_d_skip = g_skip.reshape(H, P_SIZE).sum(1)
    g_cols = g_cols[:, :, :4].reshape(pairs, count, 2, 2).transpose(2, 1, 0, 3)
    g_cols = g_cols.reshape(2, count, H)
    g_cum = g_cols[0] - g_rows.reshape(H, count).T
    g_decay = jnp.einsum(
        "ts,bth->bsh", lower, g_cum.reshape(blocks, SPAN, H), precision=HIGH
    ).reshape(count, H)
    g_step = g_cols[1] - jnp.exp(a_log)[None, :] * g_decay
    g_a_log = (g_decay * decay).sum(0)
    g_dt_raw = g_step * jax.nn.sigmoid(dt_raw + dt_bias[None, :])
    g_dt_bias = g_dt_raw.sum(0)

    g_xbc, g_rim, g_conv_w, g_conv_b = conv_pull(g_conv)
    from_next = passed_along(g_rim, "shard", -1)
    g_xbc = g_xbc + jnp.pad(from_next, ((count - rim_len, 0), (0, 0)))
    g_projected = jnp.concatenate([g_gate_z, g_xbc, g_dt_raw], axis=1).astype(jnp.bfloat16)
    grad_in_full = mm(normed_b, g_projected, TN)
    part_in = owned_sum(grad_in_full)
    g_normed = mm(g_projected, full_in, NT)
    g_tokens, g_norm_gain = norm_pull(g_normed)
    grad_tokens = cotangent.astype(jnp.float32) + g_tokens

    flat = jnp.concatenate(
        [g_conv_w.reshape(-1), g_conv_b, g_norm_gain, g_gate_gain, g_dt_bias, g_a_log, g_d_skip]
    )
    width = flat.size
    flat = jnp.pad(flat, (0, -width % 1024)).reshape(-1, N)
    flat = lax.psum(flat, ("replica", "shard")).reshape(-1)
    cuts = [0]
    for g in (g_conv_w, g_conv_b, g_norm_gain, g_gate_gain, g_dt_bias, g_a_log, g_d_skip):
        cuts.append(cuts[-1] + g.size)
    piece = [flat[a:b] for a, b in zip(cuts, cuts[1:])]
    at = lax.axis_index("shard")

    def own(v, like):
        return lax.dynamic_slice_in_dim(v, at * like.shape[-1], like.shape[-1], v.ndim - 1)

    return (
        block_out,
        grad_tokens,
        own(piece[2], norm_gain),
        part_in,
        own(piece[0].reshape(KC, -1), conv_w),
        own(piece[1], conv_b),
        piece[4],
        piece[5],
        piece[6],
        own(piece[3], gate_gain),
        part_out,
    )


def solution(mesh):
    in_specs = (
        P(("replica", "shard"), None),
        P(("replica", "shard")),
        P("shard"),
        P("shard", None),
        P(None, "shard"),
        P("shard"),
        P(),
        P(),
        P(),
        P("shard"),
        P("shard", None),
        P(("replica", "shard"), None),
    )
    out_specs = (
        P(("replica", "shard"), None),
        P(("replica", "shard"), None),
        P("shard"),
        P("shard", None),
        P(None, "shard"),
        P("shard"),
        P(),
        P(),
        P(),
        P("shard"),
        P("shard", None),
    )
    return jax.shard_map(body, mesh=mesh, in_specs=in_specs, out_specs=out_specs, check_vma=False)
```

```python
import jax
import jax.numpy as jnp
from jax import lax
from jax.experimental import pallas as pl
from jax.experimental.pallas import tpu as pltpu
from jax.sharding import PartitionSpec as P

H = 24
P_SIZE = 64
N = 128
KC = 4
SPAN = 256
DI = 1536
CONV = 1792


EPSILON = 1e-05
WRAP_IDS = 256
MAX_LEN = 4096


def passed_along(shard, axis, by):
    count = lax.axis_size(axis)
    pairs = [(i, i + by) for i in range(count) if 0 <= i + by < count]
    return lax.ppermute(shard, axis, pairs)


def rms_scale(values, gain_vec):
    return (
        values * lax.rsqrt(jnp.mean(values * values, axis=-1, keepdims=True) + EPSILON) * gain_vec
    )


def causal_conv(xbc_in, rim_in, weight_in, bias_in, segment_ids, rim_segments):
    width = weight_in.shape[0]
    length = xbc_in.shape[0]
    row_block = jnp.concatenate([rim_in, xbc_in], axis=0)
    seg_block = jnp.concatenate([rim_segments, segment_ids], axis=0)
    summed = jnp.zeros_like(xbc_in) + bias_in[None, :]
    for offset in range(width):
        kept_mask = (seg_block[offset : offset + length] == segment_ids).astype(jnp.float32)
        summed = (
            summed
            + weight_in[offset][None, :] * row_block[offset : offset + length] * kept_mask[:, None]
        )
    return jax.nn.silu(summed)


def log_decay(raw_in, bias_in, alog_in):
    step_size = jax.nn.softplus(raw_in + bias_in[None, :])
    return (step_size, -jnp.exp(alog_in)[None, :] * step_size)


def gated_norm(mixed_in, gate_in, gain_in):
    product = mixed_in * jax.nn.silu(gate_in)
    return (
        product
        * lax.rsqrt(jnp.mean(product * product, axis=-1, keepdims=True) + EPSILON)
        * gain_in[None, :]
    )


MASKED = -1e30
HIGH = lax.Precision.HIGHEST


def mm(a, b, dims):
    return lax.dot_general(
        a.astype(jnp.bfloat16),
        b.astype(jnp.bfloat16),
        (dims, ((), ())),
        preferred_element_type=jnp.float32,
    )


NN = ((1,), (0,))
NT = ((1,), (1,))
TN = ((0,), (0,))


def block_mask(segc_ref, segr_ref, reader):
    span = segc_ref.shape[0]
    at = lax.broadcasted_iota(jnp.int32, (span, span), reader)
    of = lax.broadcasted_iota(jnp.int32, (span, span), 1 - reader)
    keep = (segc_ref[:, 0:1] == segr_ref[0:1, :]) & (at >= of)
    return jnp.where(keep, 0.0, MASKED)


def pair_columns(cols, first):
    lane = lax.broadcasted_iota(jnp.int32, (cols.shape[0], 2 * P_SIZE), 1)
    return jnp.where(lane < P_SIZE, cols[:, first : first + 1], cols[:, first + 1 : first + 2])


def forward_kernel(
    conv_ref, cols_ref, rows_ref, segc_ref, segr_ref, skip_ref,
    mixed_ref, enter_ref, final_ref, state, bias, scores,
):
    span = conv_ref.shape[0]
    pairs = cols_ref.shape[0]
    wide = 2 * P_SIZE

    @pl.when(pl.program_id(0) == 0)
    def _():
        state[...] = jnp.zeros_like(state)

    b_mat = conv_ref[:, DI : DI + N]
    c_mat = conv_ref[:, DI + N :]
    bias[...] = block_mask(segc_ref, segr_ref, 0)
    scores[...] = mm(c_mat, b_mat, NT)
    enter_ref[0] = state[...]
    lane = lax.broadcasted_iota(jnp.int32, (span, wide), 1)

    @pl.loop(0, pairs)
    def _(j):
        at = pl.ds(pl.multiple_of(j * wide, wide), wide)
        cols = cols_ref[j]
        xs = conv_ref[:, at].astype(jnp.float32)
        x = xs * pair_columns(cols, 2)
        xb = x.astype(jnp.bfloat16)
        parts = []
        for a in range(2):
            gaps = cols[:, a : a + 1] - rows_ref[j, a : a + 1, :]
            w = jnp.exp(gaps + bias[...]) * scores[...]
            parts.append(mm(w, xb, NN))
        within = jnp.where(lane < P_SIZE, parts[0], parts[1])
        enter = pair_columns(cols, 4)
        old = state[at, :]
        from_state = mm(c_mat, old, NT) * enter
        mixed_ref[:, at] = within + from_state + skip_ref[:, at] * xs
        leave = pair_columns(cols, 6)
        sub = lax.broadcasted_iota(jnp.int32, (wide, N), 0)
        passing = jnp.where(sub < P_SIZE, cols[span - 1 :, 4:5], cols[span - 1 :, 5:6])
        state[at, :] = old * passing + mm(x * leave, b_mat, TN)

    final_ref[...] = state[...]


def backward_kernel(
    conv_ref, gmix_ref, cols_ref, rows_ref, segc_ref, segr_ref, skip_ref, enter_ref, gout_ref,
    gconv_ref, gcols_ref, grows_ref, gskip_ref, gstate, bias, scores, gscores, gbc,
):
    span = conv_ref.shape[0]
    pairs = cols_ref.shape[0]
    wide = 2 * P_SIZE

    @pl.when(pl.program_id(0) == 0)
    def _():
        gstate[...] = gout_ref[...]
        gskip_ref[...] = jnp.zeros_like(gskip_ref)

    b_mat = conv_ref[:, DI : DI + N]
    c_mat = conv_ref[:, DI + N :]
    bias[...] = block_mask(segc_ref, segr_ref, 1)
    scores[...] = mm(b_mat, c_mat, NT)
    gscores[...] = jnp.zeros_like(gscores)
    gbc[...] = jnp.zeros_like(gbc)
    lane = lax.broadcasted_iota(jnp.int32, (span, wide), 1)
    low = lane < P_SIZE
    low_sub = lax.broadcasted_iota(jnp.int32, (wide, N), 0) < P_SIZE
    last = lax.broadcasted_iota(jnp.int32, (span, 1), 0) == span - 1
    lane8 = lax.broadcasted_iota(jnp.int32, (span, 8), 1)

    @pl.loop(0, pairs)
    def _(j):
        at = pl.ds(pl.multiple_of(j * wide, wide), wide)
        cols = cols_ref[j]
        xs = conv_ref[:, at].astype(jnp.float32)
        dt = pair_columns(cols, 2)
        x = xs * dt
        xb = x.astype(jnp.bfloat16)
        gy = gmix_ref[:, at]
        gyb = gy.astype(jnp.bfloat16)
        parts = []
        col_sums = []
        for a in range(2):
            gaps = rows_ref[j, a : a + 1, :] - cols[:, a : a + 1]
            e = jnp.exp(gaps + bias[...])
            w = e * scores[...]
            mine = low if a == 0 else jnp.logical_not(low)
            dw = mm(xb, jnp.where(mine, gy, 0.0), NT)
            gscores[...] += e * dw
            q = w * dw
            col_sums.append(jnp.sum(q, axis=1, keepdims=True))
            grows_ref[j, a : a + 1, :] = jnp.sum(q, axis=0, keepdims=True)
            parts.append(mm(w, gyb, NN))
        gx = jnp.where(low, parts[0], parts[1])
        enter = pair_columns(cols, 4)
        leave = pair_columns(cols, 6)
        old = enter_ref[0, at, :]
        late = gstate[at, :]
        gye = gy * enter
        from_state = mm(c_mat, old, NT)
        gx_late = mm(b_mat, late, NT) * leave
        gbc[:, N:] += mm(gye, old, NN)
        gbc[:, :N] += mm(x * leave, late, NN)
        gx = gx + gx_late
        late_term = x * gx_late
        v1 = gye * from_state - late_term
        v2 = gx * xs
        passing = jnp.where(low_sub, cols[span - 1 :, 4:5], cols[span - 1 :, 5:6])
        through = late * passing
        kept = jnp.sum(through * old, axis=1, keepdims=True)
        ends = jnp.sum(late_term, axis=0, keepdims=True)
        low_row = lax.broadcasted_iota(jnp.int32, (1, wide), 1) < P_SIZE
        out = jnp.zeros((span, 8), jnp.float32)
        for a in range(2):
            mine = low if a == 0 else jnp.logical_not(low)
            mine_row = low_row if a == 0 else jnp.logical_not(low_row)
            tail = jnp.sum(jnp.where(mine_row, ends, 0.0), axis=1, keepdims=True)
            tail = tail + jnp.sum(
                kept[a * P_SIZE : (a + 1) * P_SIZE], axis=0, keepdims=True
            )
            gcum = jnp.sum(jnp.where(mine, v1, 0.0), axis=1, keepdims=True) - col_sums[a]
            gcum = gcum + jnp.where(last, tail, 0.0)
            gdt = jnp.sum(jnp.where(mine, v2, 0.0), axis=1, keepdims=True)
            out = jnp.where(lane8 == a, gcum, out)
            out = jnp.where(lane8 == 2 + a, gdt, out)
        gcols_ref[j] = out
        gskip_ref[:, at] += jnp.sum(gy * xs, axis=0, keepdims=True)
        gconv_ref[:, at] = gx * dt + skip_ref[:, at] * gy
        gstate[at, :] = through + mm(gye, c_mat, TN)

    gs = gscores[...].astype(jnp.bfloat16)
    gconv_ref[:, DI : DI + N] = gbc[:, :N] + mm(gs, c_mat, NN)
    gconv_ref[:, DI + N :] = gbc[:, N:] + mm(gs, b_mat, TN)


def scan_specs(count, order):
    pairs = H // 2
    return dict(
        conv=pl.BlockSpec((SPAN, CONV), lambda i: (order(i), 0)),
        mix=pl.BlockSpec((SPAN, DI), lambda i: (order(i), 0)),
        cols=pl.BlockSpec((pairs, SPAN, 8), lambda i: (0, order(i), 0)),
        rows=pl.BlockSpec((pairs, 2, SPAN), lambda i: (0, 0, order(i))),
        segc=pl.BlockSpec((SPAN, 1), lambda i: (order(i), 0)),
        segr=pl.BlockSpec((1, SPAN), lambda i: (0, order(i))),
        skip=pl.BlockSpec((1, DI), lambda i: (0, 0)),
        state=pl.BlockSpec((DI, N), lambda i: (0, 0)),
        states=pl.BlockSpec((1, DI, N), lambda i: (order(i), 0, 0)),
    )


def scan_forward(conv_b, cols, rows, segc, segr, skip):
    length = conv_b.shape[0]
    count = length // SPAN
    s = scan_specs(count, lambda i: i)
    f32 = jnp.float32
    return pl.pallas_call(
        forward_kernel,
        grid=(count,),
        in_specs=[s["conv"], s["cols"], s["rows"], s["segc"], s["segr"], s["skip"]],
        out_specs=[s["mix"], s["states"], s["state"]],
        out_shape=[
            jax.ShapeDtypeStruct((length, DI), f32),
            jax.ShapeDtypeStruct((count, DI, N), f32),
            jax.ShapeDtypeStruct((DI, N), f32),
        ],
        scratch_shapes=[
            pltpu.VMEM((DI, N), f32),
            pltpu.VMEM((SPAN, SPAN), f32),
            pltpu.VMEM((SPAN, SPAN), f32),
        ],
        compiler_params=pltpu.CompilerParams(vmem_limit_bytes=48 << 20),
    )(conv_b, cols, rows, segc, segr, skip)


def scan_backward(conv_b, g_mixed, cols, rows, segc, segr, skip, states, g_out):
    length = conv_b.shape[0]
    count = length // SPAN
    s = scan_specs(count, lambda i: count - 1 - i)
    f32 = jnp.float32
    return pl.pallas_call(
        backward_kernel,
        grid=(count,),
        in_specs=[
            s["conv"], s["mix"], s["cols"], s["rows"], s["segc"], s["segr"], s["skip"],
            s["states"], s["state"],
        ],
        out_specs=[s["conv"], s["cols"], s["rows"], s["skip"]],
        out_shape=[
            jax.ShapeDtypeStruct((length, CONV), f32),
            jax.ShapeDtypeStruct(cols.shape, f32),
            jax.ShapeDtypeStruct(rows.shape, f32),
            jax.ShapeDtypeStruct((1, DI), f32),
        ],
        scratch_shapes=[
            pltpu.VMEM((DI, N), f32),
            pltpu.VMEM((SPAN, SPAN), f32),
            pltpu.VMEM((SPAN, SPAN), f32),
            pltpu.VMEM((SPAN, SPAN), f32),
            pltpu.VMEM((SPAN, 2 * N), f32),
        ],
        compiler_params=pltpu.CompilerParams(vmem_limit_bytes=48 << 20),
    )(conv_b, g_mixed, cols, rows, segc, segr, skip, states, g_out)


def carried(state, gain, reverse, tokens_here):
    reach = min(lax.axis_size("shard") - 1, -(-MAX_LEN // tokens_here))
    sign = -1 if reverse else 1

    def arriving(state, gain, by):
        tail = jnp.pad(gain[None, :], ((0, 15), (0, N - H)))
        sent = jnp.concatenate([state, tail], axis=0).astype(jnp.bfloat16)
        got = passed_along(sent, "shard", sign * by).astype(jnp.float32)
        return got[:DI], got[DI, :H]

    covered = 1
    while covered < reach:
        far_state, far_gain = arriving(state, gain, covered)
        state = far_state * jnp.repeat(gain, P_SIZE)[:, None] + state
        gain = far_gain * gain
        covered *= 2
    return arriving(state, gain, 1)[0]


def gather_params(w_in, w_out, conv_w, conv_b, norm_gain, gate_gain):
    parts = lax.axis_size("replica")
    mine = lax.axis_index("replica")

    def whole(w):
        rows = w.shape[0] // parts
        part = lax.dynamic_slice_in_dim(w, mine * rows, rows, 0)
        return lax.all_gather(part, ("shard", "replica"), axis=0, tiled=True)

    small = jnp.concatenate([conv_w.reshape(-1), conv_b, norm_gain, gate_gain])
    small = lax.all_gather(small, "shard", axis=0)
    count = small.shape[0]
    a = conv_w.size
    b = a + conv_b.size
    c = b + norm_gain.size
    full_conv = small[:, :a].reshape(count, KC, -1).transpose(1, 0, 2).reshape(KC, -1)
    return (
        whole(w_in[:, DI:]),
        whole(w_in[:, :DI]),
        whole(w_out),
        full_conv.astype(jnp.float32),
        small[:, a:b].reshape(-1).astype(jnp.float32),
        small[:, b:c].reshape(-1).astype(jnp.float32),
        small[:, c:].reshape(-1).astype(jnp.float32),
    )


def owned_sum(g):
    part = lax.psum_scatter(
        g.astype(jnp.bfloat16), ("shard", "replica"), scatter_dimension=0, tiled=True
    )
    return lax.all_gather(part, "replica", axis=0, tiled=True).astype(jnp.float32)


def body(
    tokens,
    segment,
    norm_gain,
    w_in,
    conv_w,
    conv_b,
    dt_bias,
    a_log,
    d_skip,
    gate_gain,
    w_out,
    cotangent,
):
    in_rest, in_z, full_out, full_conv, full_bias, full_norm, full_gate = gather_params(
        w_in, w_out, conv_w, conv_b, norm_gain, gate_gain
    )
    rim_len = KC - 1
    wrapped = segment % WRAP_IDS
    tok_f = tokens.astype(jnp.float32)
    count = tokens.shape[0]
    blocks = count // SPAN

    def norm_piece(tok_in, gain_in):
        return rms_scale(tok_in, gain_in[None, :])

    normed, norm_pull = jax.vjp(norm_piece, tok_f, full_norm)
    normed_b = normed.astype(jnp.bfloat16)
    projected = mm(normed_b, in_rest, NN).astype(jnp.bfloat16)
    xbc_b = projected[:, :CONV]
    rim = jnp.concatenate(
        [
            xbc_b[-rim_len:],
            jnp.broadcast_to(wrapped[-rim_len:, None].astype(jnp.bfloat16), (rim_len, N)),
        ],
        axis=1,
    )
    rim = passed_along(rim, "shard", 1)
    rim_rows = rim[:, :CONV]
    prev_segs = rim[:, CONV].astype(jnp.int32)
    prev_last = jnp.where(lax.axis_index("shard") == 0, 0, prev_segs[-1])
    xbc_f = xbc_b.astype(jnp.float32)
    rim_f = rim_rows.astype(jnp.float32)
    dt_raw = projected[:, CONV:].astype(jnp.float32)

    def conv_piece(xbc_in, rim_in, weight_in, bias_in):
        return causal_conv(xbc_in, rim_in, weight_in, bias_in, wrapped, prev_segs)

    conv_out, conv_pull = jax.vjp(conv_piece, xbc_f, rim_f, full_conv, full_bias)
    conv_bf = conv_out.astype(jnp.bfloat16)

    step, decay = log_decay(dt_raw, dt_bias, a_log)
    decay_blocks = decay.reshape(blocks, SPAN, H)
    lower = jnp.tril(jnp.ones((SPAN, SPAN), jnp.float32))
    cum_blocks = jnp.einsum("ts,bsh->bth", lower, decay_blocks, precision=HIGH)
    seg_blocks = wrapped.reshape(blocks, SPAN)
    ends = seg_blocks[:, -1]
    before = jnp.concatenate([prev_last[None], ends[:-1]])
    at_last = cum_blocks[:, -1:]
    enter = jnp.exp(cum_blocks) * (seg_blocks == before[:, None]).astype(jnp.float32)[:, :, None]
    leave = (
        jnp.exp(at_last - cum_blocks)
        * (seg_blocks == ends[:, None]).astype(jnp.float32)[:, :, None]
    )
    before_sum = [jnp.zeros((H,), jnp.float32)]
    for b in range(blocks):
        before_sum.append(before_sum[-1] + cum_blocks[b, -1])
    base = jnp.stack(before_sum[:-1])
    running = (
        jnp.exp(cum_blocks + base[:, None, :]).reshape(count, H)
        * (wrapped == prev_last).astype(jnp.float32)[:, None]
    )
    carry_gain = running[-1]
    entering_gain = jnp.concatenate(
        [jnp.ones((1, H), jnp.float32), running.reshape(blocks, SPAN, H)[:-1, -1]]
    )

    pairs = H // 2
    cols = jnp.stack(
        [cum_blocks.reshape(count, H), step, enter.reshape(count, H), leave.reshape(count, H)],
        axis=1,
    )
    cols = cols.reshape(count, 4, pairs, 2).transpose(2, 0, 1, 3).reshape(pairs, count, 8)
    rows = cum_blocks.reshape(count, pairs, 2).transpose(1, 2, 0)
    segc = wrapped[:, None]
    segr = wrapped[None, :]
    skip = jnp.repeat(d_skip, P_SIZE)[None, :]

    local_mixed, local_states, local_state = scan_forward(conv_bf, cols, rows, segc, segr, skip)
    local_state, in_z = lax.optimization_barrier((local_state, in_z))
    gate_z = mm(normed_b, in_z, NN).astype(jnp.bfloat16).astype(jnp.float32)
    state_in = carried(local_state, carry_gain, False, count)
    state_in, full_out = lax.optimization_barrier((state_in, full_out))
    c_mat = conv_bf[:, DI + N :]
    running_wide = jnp.repeat(running, P_SIZE, axis=1)
    mixed_out = local_mixed + mm(c_mat, state_in, NT) * running_wide
    gated_out, gate_pull = jax.vjp(gated_norm, mixed_out, gate_z, full_gate)
    gated_b = gated_out.astype(jnp.bfloat16)
    branch = jnp.dot(gated_b, full_out, preferred_element_type=jnp.float32)
    block_out = (tok_f + branch).astype(jnp.bfloat16)

    g_gated = mm(cotangent, full_out, NT)
    grad_out_full = mm(gated_b, cotangent, TN)
    part_out = owned_sum(grad_out_full)
    g_mixed, g_gate_z, g_gate_gain = gate_pull(g_gated)
    g_z_b = g_gate_z.astype(jnp.bfloat16)
    part_z = owned_sum(mm(normed_b, g_z_b, TN))
    seed_grad = mm(g_mixed * running_wide, c_mat, TN)
    state_out_grad = carried(seed_grad, carry_gain, True, count)
    states = (
        local_states
        + jnp.repeat(entering_gain, P_SIZE, axis=1)[:, :, None] * state_in[None]
    )
    g_conv, g_cols, g_rows, g_skip = scan_backward(
        conv_bf, g_mixed, cols, rows, segc, segr, skip, states, state_out_grad
    )
    g_d_skip = g_skip.reshape(H, P_SIZE).sum(1)
    g_cols = g_cols[:, :, :4].reshape(pairs, count, 2, 2).transpose(2, 1, 0, 3)
    g_cols = g_cols.reshape(2, count, H)
    g_cum = g_cols[0] + g_rows.reshape(H, count).T
    g_decay = jnp.einsum(
        "ts,bth->bsh", lower, g_cum.reshape(blocks, SPAN, H), precision=HIGH
    ).reshape(count, H)
    g_step = g_cols[1] - jnp.exp(a_log)[None, :] * g_decay
    g_a_log = (g_decay * decay).sum(0)
    g_dt_raw = g_step * jax.nn.sigmoid(dt_raw + dt_bias[None, :])
    g_dt_bias = g_dt_raw.sum(0)

    g_xbc, g_rim, g_conv_w, g_conv_b = conv_pull(g_conv)
    from_next = passed_along(g_rim, "shard", -1)
    g_xbc = g_xbc + jnp.pad(from_next, ((count - rim_len, 0), (0, 0)))
    g_projected = jnp.concatenate([g_xbc, g_dt_raw], axis=1).astype(jnp.bfloat16)
    grad_in_full = mm(normed_b, g_projected, TN)
    part_in = jnp.concatenate([part_z, owned_sum(grad_in_full)], axis=1)
    g_normed = mm(g_projected, in_rest, NT) + mm(g_z_b, in_z, NT)
    g_tokens, g_norm_gain = norm_pull(g_normed)
    grad_tokens = cotangent.astype(jnp.float32) + g_tokens

    flat = jnp.concatenate(
        [g_conv_w.reshape(-1), g_conv_b, g_norm_gain, g_gate_gain, g_dt_bias, g_a_log, g_d_skip]
    )
    width = flat.size
    flat = jnp.pad(flat, (0, -width % 1024)).reshape(-1, N)
    flat = lax.psum(flat, ("replica", "shard")).reshape(-1)
    cuts = [0]
    for g in (g_conv_w, g_conv_b, g_norm_gain, g_gate_gain, g_dt_bias, g_a_log, g_d_skip):
        cuts.append(cuts[-1] + g.size)
    piece = [flat[a:b] for a, b in zip(cuts, cuts[1:])]
    at = lax.axis_index("shard")

    def own(v, like):
        return lax.dynamic_slice_in_dim(v, at * like.shape[-1], like.shape[-1], v.ndim - 1)

    return (
        block_out,
        grad_tokens,
        own(piece[2], norm_gain),
        part_in,
        own(piece[0].reshape(KC, -1), conv_w),
        own(piece[1], conv_b),
        piece[4],
        piece[5],
        piece[6],
        own(piece[3], gate_gain),
        part_out,
    )


def solution(mesh):
    in_specs = (
        P(("replica", "shard"), None),
        P(("replica", "shard")),
        P("shard"),
        P("shard", None),
        P(None, "shard"),
        P("shard"),
        P(),
        P(),
        P(),
        P("shard"),
        P("shard", None),
        P(("replica", "shard"), None),
    )
    out_specs = (
        P(("replica", "shard"), None),
        P(("replica", "shard"), None),
        P("shard"),
        P("shard", None),
        P(None, "shard"),
        P("shard"),
        P(),
        P(),
        P(),
        P("shard"),
        P("shard", None),
    )
    return jax.shard_map(body, mesh=mesh, in_specs=in_specs, out_specs=out_specs, check_vma=False)
```
